256 devices in a mesh: row: 16 (over y, x), col: 16 (over z, core).
Axes of the slice: x: 4, y: 4, z: 8, core: 2. Of those that a mesh axis runs over, the one named last changes fastest.
Arguments:
- tokens: bfloat16 [1024, 8192], P('col', 'row'), may hold values from -6 to 6
- out_grad: bfloat16 [1024, 8192], P('col', 'row'), may hold values from -6 to 6
- w_gate: bfloat16 [8192, 28672], P('row', 'col'), may hold values from -0.0625 to 0.0625
- w_up: bfloat16 [8192, 28672], P('row', 'col'), may hold values from -0.0625 to 0.0625
- w_down: bfloat16 [28672, 8192], P('col', 'row'), may hold values from -0.0625 to 0.0625
Outputs:
- in_grad: bfloat16 [1024, 8192], P('col', 'row')
- gate_grad: bfloat16 [8192, 28672], P('row', 'col')
- up_grad: bfloat16 [8192, 28672], P('row', 'col')
- down_grad: bfloat16 [28672, 8192], P('col', 'row')
The draws below stay inside these ranges and needn't reach their ends.
All inputs are finite; a program needn't handle non-finite values.
Results may differ from the reference program's by a relative error of at most 0.035.
Values may be sent and summed in bfloat16 or wider, within the bound.
A program may use at most 128 MiB of HBM per device.

```python
import jax
import jax.numpy as jnp
from jax import lax

D = 8192
FF = 28672
TOKENS = 1024
N_ROW = 16


def spiked(result, stream_key, source, target, shards_of, factor):
    owner, partner = [(jnp.arange(result.shape[axis_at]) // (result.shape[axis_at] // shards_of)).reshape([-1 if axis == axis_at else 1 for axis in range(result.ndim)]) for axis_at in (source, target)]
    chosen = jax.random.permutation(stream_key, shards_of)[partner]
    strong = (owner == chosen) | (owner == (partner + shards_of // 2) % shards_of)
    return jnp.where(strong, factor * result, result)


def block_levels(key, shape, split, low, top_value):
    level, own = 1.0, jax.random.fold_in(key, 6)
    for axis_at, blocks in split:
        draws = jnp.exp(jax.random.uniform(jax.random.fold_in(own, axis_at), (blocks,), jnp.float32, low / len(split), top_value / len(split)))
        level = level * jnp.repeat(draws, shape[axis_at] // blocks).reshape([-1 if axis == axis_at else 1 for axis in range(len(shape))])
    return level


def gaussian(stream_key, shape, scale, most, split=(), kind=jnp.bfloat16):
    result = scale * jax.random.normal(stream_key, shape, jnp.float32)
    if split:
        result = result * block_levels(stream_key, shape, split, -0.22, 0.18)
    return jnp.clip(result, -most, most).astype(kind)


def bell_draw_with(own_key, shape, scale, most, pieces, heavy, dtype=jnp.bfloat16):
    result = scale * jax.random.normal(own_key, shape, jnp.float32)
    if pieces:
        result = result * block_levels(own_key, shape, pieces, -0.22, 0.18)
    return jnp.clip(spiked(result, jax.random.fold_in(own_key, 3), *heavy), -most, most).astype(dtype)


def setup_inputs(seed: int = 0) -> dict:
    key_of = jax.random.split(jax.random.key(seed), 6)
    tokens = bell_draw_with(key_of[0], (TOKENS, D), 1.0, 6.0, ((0, 16), (1, 16)), (1, 0, 16, 2.0))
    out_grad = bell_draw_with(key_of[1], (TOKENS, D), 1.0, 6.0, ((0, 16), (1, 16)), (1, 0, 16, 2.0))
    w_gate = gaussian(key_of[2], (D, FF), D ** -0.5, 0.0625, ((0, 16), (1, 16)))
    w_up = gaussian(key_of[3], (D, FF), D ** -0.5, 0.0625, ((0, 16), (1, 16)))
    w_down = gaussian(key_of[4], (FF, D), D ** -0.5, 0.0625, ((0, 16), (1, 16)))
    return dict(tokens=tokens, out_grad=out_grad, w_gate=w_gate, w_up=w_up, w_down=w_down)


def block_sum(left, right, contract_right):
    blocks = N_ROW
    width = left.shape[1] // blocks
    total = None
    for index in range(blocks):
        piece = left[:, index * width:(index + 1) * width]
        if contract_right == 0:
            weight = right[index * width:(index + 1) * width, :]
            term = lax.dot_general(piece, weight, (((1,), (0,)), ((), ())), preferred_element_type=jnp.float32)
        else:
            weight = right[:, index * width:(index + 1) * width]
            term = lax.dot_general(piece, weight, (((1,), (1,)), ((), ())), preferred_element_type=jnp.float32)
        term = term.astype(jnp.bfloat16).astype(jnp.float32)
        total = term if total is None else total + term
    return total.astype(jnp.bfloat16)


def reference(tokens, out_grad, w_gate, w_up, w_down):
    gate = block_sum(tokens, w_gate, 0)
    upval = block_sum(tokens, w_up, 0)
    dhid = block_sum(out_grad, w_down, 1).astype(jnp.float32)
    g_val = gate.astype(jnp.float32)
    u_val = upval.astype(jnp.float32)
    sig = jax.nn.sigmoid(g_val)
    hidden = (g_val * sig * u_val).astype(jnp.bfloat16)
    dgate = (dhid * u_val * sig * (1.0 + g_val * (1.0 - sig))).astype(jnp.bfloat16)
    dup = (dhid * g_val * sig).astype(jnp.bfloat16)
    rows_dims = (((0,), (0,)), ((), ()))
    down_grad = lax.dot_general(hidden, out_grad, rows_dims, preferred_element_type=jnp.float32).astype(jnp.bfloat16)
    gate_grad = lax.dot_general(tokens, dgate, rows_dims, preferred_element_type=jnp.float32).astype(jnp.bfloat16)
    up_grad = lax.dot_general(tokens, dup, rows_dims, preferred_element_type=jnp.float32).astype(jnp.bfloat16)
    cols_dims = (((1,), (1,)), ((), ()))
    in_grad = lax.dot_general(dgate, w_gate, cols_dims, preferred_element_type=jnp.float32)
    in_grad = in_grad + lax.dot_general(dup, w_up, cols_dims, preferred_element_type=jnp.float32)
    return in_grad.astype(jnp.bfloat16), gate_grad, up_grad, down_grad
```

```python
import functools

import jax
import jax.numpy as jnp
from jax import lax
from jax.experimental import pallas as pl
from jax.experimental.pallas import tpu as pltpu
from jax.sharding import PartitionSpec as P

MESH = pl.DeviceIdType.MESH
BF = jnp.bfloat16
F32 = jnp.float32

RING = 4
CHIPS = 8
CORES = 2
CHUNKS = 4
OWN = 64
SUB = 16
WIDTH = 512
HID = 1792
HALF = HID // 2
CAT = 3 * HALF
TOKENS = 1024

ORDER = (
    ("first", 0), ("fwd", 1), ("part", 1), ("rs_a1", 0), ("fwd", 2), ("part", 2), ("rs_a2", 0),
    ("rs_a1", 1), ("fwd", 3), ("rs_b1", 0), ("part", 3), ("rs_b2", 0), ("rs_a2", 1), ("ag_b1", 0),
    ("rs_a1", 2), ("rs_b1", 1), ("ag_b2", 0), ("rs_b2", 1), ("rs_a2", 2), ("rs_a1", 3), ("ag_b1", 1),
    ("ag_a1", 0), ("rs_b1", 2), ("ag_b2", 1), ("rs_b2", 2), ("rs_a2", 3), ("ag_a2", 0), ("ag_b1", 2),
    ("rs_b1", 3), ("in_part", 0), ("ag_a1", 1), ("ag_b2", 2), ("rs_b2", 3), ("in_send", 0), ("ag_b1", 3),
    ("ag_a2", 1), ("ag_b2", 3), ("in_part", 1), ("ag_a1", 2), ("in_send", 1), ("ag_a2", 2), ("ag_a1", 3),
    ("in_part", 2), ("in_send", 2), ("ag_a2", 3), ("in_part", 3),
)


def dot(left, right, dims):
    return lax.dot_general(left, right, (dims, ((), ())), preferred_element_type=F32)


def kernel(
    tok_in, grd_in, wg_in, wu_in, wd_in, ing_ref, gg_ref, ug_ref, dg_ref,
    tok, grd, tok_t, hid_t, wg, wu, wd, part, gath, relay_a, land_a, relay_b, land_b,
    in_own, in_sib, in_far, out_g, out_u, out_d,
    load_sem, z_send, z_recv, f_send, f_recv, send, recv, i_send, i_recv, j_send, j_recv, out_sem,
):
    row, col = lax.axis_index("row"), lax.axis_index("col")
    x, y = row % RING, row // RING
    z, core = col // CORES, col % CORES
    pa, pb = x + core * (y - x), y + core * (x - y)
    step_a, step_b = 1 + 3 * core, RING - 3 * core

    def at(a, b):
        return (a * step_a + b * step_b, col)

    up_a, down_a, opp_a = (pa + 1) % RING, (pa + 3) % RING, (pa + 2) % RING
    up_b, down_b, opp_b = (pb + 1) % RING, (pb + 3) % RING, (pb + 2) % RING
    dev_up_a, dev_down_a = at(up_a, pb), at(down_a, pb)
    dev_up_b, dev_down_b = at(pa, up_b), at(pa, down_b)
    sibling = (row, z * CORES + 1 - core)

    def far(step):
        return (row, ((z + step) % CHIPS) * CORES + core)

    loads = [
        pltpu.make_async_copy(tok_in, tok.at[0, core], load_sem.at[0]),
        pltpu.make_async_copy(grd_in, grd.at[0, core], load_sem.at[1]),
        pltpu.make_async_copy(wg_in, wg, load_sem.at[2]),
        pltpu.make_async_copy(wu_in, wu, load_sem.at[3]),
        pltpu.make_async_copy(wd_in, wd, load_sem.at[4]),
    ]
    for copy in loads:
        copy.start()

    barrier = pltpu.get_barrier_semaphore()
    peers = [dev_up_a, dev_down_a, dev_up_b, dev_down_b, sibling] + [far(s) for s in range(1, CHIPS)]
    for peer in peers:
        pl.semaphore_signal(barrier, inc=1, device_id=peer, device_id_type=MESH)
    pl.semaphore_wait(barrier, len(peers))

    started = []

    def push(src, dst, send_sem, recv_sem, device):
        copy = pltpu.make_async_remote_copy(
            src_ref=src, dst_ref=dst, send_sem=send_sem, recv_sem=recv_sem,
            device_id=device, device_id_type=MESH,
        )
        copy.start()
        started.append(copy)
        return copy

    from_sib, from_far = {}, {}

    def to_sibling(slot, src_tok, src_grd):
        from_sib[slot] = [
            push(src_tok, tok.at[slot, core], f_send.at[slot, 0], f_recv.at[slot, 0], sibling),
            push(src_grd, grd.at[slot, core], f_send.at[slot, 1], f_recv.at[slot, 1], sibling),
        ]

    def to_far(slot):
        device = far(CHIPS - slot)
        from_far[slot] = [
            push(tok_in, tok.at[slot, core], z_send.at[slot, 0], z_recv.at[slot, 0], device),
            push(grd_in, grd.at[slot, core], z_send.at[slot, 1], z_recv.at[slot, 1], device),
        ]

    to_far(1)
    to_sibling(0, tok_in, grd_in)
    for slot in (2, 7, 3, 6, 4, 5):
        to_far(slot)

    def forward(slot):
        for copy in from_far[slot]:
            copy.wait_recv()
        to_sibling(slot, tok.at[slot, core], grd.at[slot, core])

    def settle(slot):
        for copy in from_sib[slot]:
            copy.wait_recv()

    def partial(j, slot, count):
        rows = count * CORES * OWN
        blocks = rows // (RING * SUB)
        first = (slot - 2 * j) * 2
        tokens = tok[slot:slot + count].reshape(rows, WIDTH)
        grads = grd[slot:slot + count].reshape(rows, WIDTH)
        tok_t[:, slot * 128:slot * 128 + rows] = tokens.T
        for h in range(2):
            cols = slice(h * HALF, (h + 1) * HALF)

            def put(place, value):
                part[j, h, first:first + blocks, :, :, place * HALF:(place + 1) * HALF] = value.astype(
                    BF).reshape(blocks, RING, SUB, HALF)

            put(0, dot(tokens, wg[:, cols], ((1,), (0,))))
            put(1, dot(tokens, wu[:, cols], ((1,), (0,))))
            put(2, dot(grads, wd[cols, :], ((1,), (1,))))

    def scatter_start(j, base, view, relay, land, me_up, me_down, me_opp, to_up, to_down):
        return {
            "r0": push(view(0, me_opp), relay.at[j, 0], send.at[j, base], recv.at[j, base], to_up),
            "r1": push(view(1, me_opp), relay.at[j, 1], send.at[j, base + 1], recv.at[j, base + 1], to_down),
            "u1": push(view(1, me_up), land.at[j, 0, 1], send.at[j, base + 2], recv.at[j, base + 2], to_up),
            "d0": push(view(0, me_down), land.at[j, 1, 0], send.at[j, base + 3], recv.at[j, base + 3], to_down),
        }

    def scatter_relay(j, base, copies, view, add, land, me_up, me_down, to_up, to_down):
        copies["r0"].wait_recv()
        add(0, me_up)
        copies["u0"] = push(view(0, me_up), land.at[j, 0, 0], send.at[j, base + 4], recv.at[j, base + 4], to_up)
        copies["r1"].wait_recv()
        add(1, me_down)
        copies["d1"] = push(view(1, me_down), land.at[j, 1, 1], send.at[j, base + 5], recv.at[j, base + 5], to_down)

    def settle_scatter(copies):
        for name in ("u1", "d0", "u0", "d1"):
            copies[name].wait_recv()

    def gather_start(j, base, view, to_up, to_down):
        return {
            "u0": push(view(0), view(0), send.at[j, base], recv.at[j, base], to_up),
            "d1": push(view(1), view(1), send.at[j, base + 1], recv.at[j, base + 1], to_down),
            "u1": push(view(1), view(1), send.at[j, base + 2], recv.at[j, base + 2], to_up),
            "d0": push(view(0), view(0), send.at[j, base + 3], recv.at[j, base + 3], to_down),
        }

    def gather_relay(j, base, copies, view_down, view_up, to_up, to_down):
        copies["u0"].wait_recv()
        copies["f0"] = push(view_down(0), view_down(0), send.at[j, base + 4], recv.at[j, base + 4], to_up)
        copies["d1"].wait_recv()
        copies["f1"] = push(view_up(1), view_up(1), send.at[j, base + 5], recv.at[j, base + 5], to_down)

    def settle_gather(copies):
        for name in ("u1", "d0", "f0", "f1"):
            copies[name].wait_recv()

    state = {}

    def view_a(j):
        return lambda h, block: part.at[j, h, block]

    def view_b(j):
        return lambda h, block: part.at[j, h, pa, block]

    def begin(j):
        state["ra", j] = scatter_start(
            j, 0, view_a(j), relay_a, land_a, up_a, down_a, opp_a, dev_up_a, dev_down_a)

    def op_first(j):
        for copy in loads:
            copy.wait()
        settle(0)
        partial(0, 0, 1)
        forward(1)
        settle(1)
        partial(0, 1, 1)
        begin(0)

    def op_fwd(j):
        forward(2 * j)
        forward(2 * j + 1)

    def op_part(j):
        settle(2 * j)
        settle(2 * j + 1)
        partial(j, 2 * j, 2)
        begin(j)

    def op_rs_a1(j):
        def add(h, block):
            def some(i, carry):
                total = part[j, h, block, i].astype(F32) + relay_a[j, h, i].astype(F32)
                part[j, h, block, i] = total.astype(BF)
                return carry
            lax.fori_loop(0, RING, some, 0)
        scatter_relay(j, 0, state["ra", j], view_a(j), add, land_a, up_a, down_a, dev_up_a, dev_down_a)

    def op_rs_a2(j):
        settle_scatter(state["ra", j])
        for h in range(2):
            def some(i, carry):
                total = part[j, h, pa, i].astype(F32) + land_a[j, 0, h, i].astype(F32)
                part[j, h, pa, i] = (total + land_a[j, 1, h, i].astype(F32)).astype(BF)
                return carry
            lax.fori_loop(0, RING, some, 0)
        state["rb", j] = scatter_start(
            j, 6, view_b(j), relay_b, land_b, up_b, down_b, opp_b, dev_up_b, dev_down_b)

    def op_rs_b1(j):
        def add(h, block):
            total = part[j, h, pa, block].astype(F32) + relay_b[j, h].astype(F32)
            part[j, h, pa, block] = total.astype(BF)
        scatter_relay(j, 6, state["rb", j], view_b(j), add, land_b, up_b, down_b, dev_up_b, dev_down_b)

    def op_rs_b2(j):
        settle_scatter(state["rb", j])
        for h in range(2):
            def total(place):
                cols = slice(place * HALF, (place + 1) * HALF)
                value = part[j, h, pa, pb, :, cols].astype(F32) + land_b[j, 0, h, :, cols].astype(F32)
                value = value + land_b[j, 1, h, :, cols].astype(F32)
                return value.astype(BF).astype(F32)
            g_val, u_val, d_val = total(0), total(1), total(2)
            sig = 1.0 / (1.0 + jnp.exp(-g_val))
            act = g_val * sig
            gath[h, j, pa, pb, :, 0:HALF] = (act * u_val).astype(BF)
            gath[h, j, pa, pb, :, HALF:2 * HALF] = (d_val * u_val * sig * (1.0 + g_val * (1.0 - sig))).astype(BF)
            gath[h, j, pa, pb, :, 2 * HALF:] = (d_val * act).astype(BF)
        state["gb", j] = gather_start(j, 12, lambda h: gath.at[h, j, pa, pb], dev_up_b, dev_down_b)

    def op_ag_b1(j):
        gather_relay(
            j, 12, state["gb", j], lambda h: gath.at[h, j, pa, down_b], lambda h: gath.at[h, j, pa, up_b],
            dev_up_b, dev_down_b)

    def op_ag_b2(j):
        settle_gather(state["gb", j])
        state["ga", j] = gather_start(j, 18, lambda h: gath.at[h, j, pa], dev_up_a, dev_down_a)

    def op_ag_a1(j):
        gather_relay(
            j, 18, state["ga", j], lambda h: gath.at[h, j, down_a], lambda h: gath.at[h, j, up_a],
            dev_up_a, dev_down_a)

    def op_ag_a2(j):
        settle_gather(state["ga", j])

    def op_in_part(j):
        total = None
        for h in range(2):
            cols = slice(h * HALF, (h + 1) * HALF)
            for place, weight in ((1, wg), (2, wu)):
                value = gath[h, j, :, :, :, place * HALF:(place + 1) * HALF].reshape(256, HALF)
                term = dot(value, weight[:, cols], ((1,), (1,)))
                total = term if total is None else total + term
        in_own[2 * j:2 * j + 2] = total.astype(BF).reshape(2, CORES, OWN, WIDTH)
        state["is", j] = push(
            in_own.at[2 * j:2 * j + 2, 1 - core], in_sib.at[2 * j:2 * j + 2], i_send.at[j], i_recv.at[j], sibling)
        for h in range(2):
            hid_t[h, :, j * 256:(j + 1) * 256] = gath[h, j, :, :, :, 0:HALF].reshape(256, HALF).T

    def op_in_send(j):
        state["is", j].wait_recv()
        for slot in (2 * j, 2 * j + 1):
            value = in_own[slot, core].astype(F32) + in_sib[slot].astype(F32)
            in_own[slot, core] = value.astype(BF)
            if slot:
                state["iz", slot] = push(
                    in_own.at[slot, core], in_far.at[slot], j_send.at[slot], j_recv.at[slot], far(slot))

    ops = dict(
        first=op_first, fwd=op_fwd, part=op_part, rs_a1=op_rs_a1, rs_a2=op_rs_a2, rs_b1=op_rs_b1, rs_b2=op_rs_b2,
        ag_b1=op_ag_b1, ag_b2=op_ag_b2, ag_a1=op_ag_a1, ag_a2=op_ag_a2, in_part=op_in_part, in_send=op_in_send,
    )
    for name, j in ORDER:
        ops[name](j)

    outs = []

    def put_out(src, dst, sem):
        copy = pltpu.make_async_copy(src, dst, sem)
        copy.start()
        outs.append(copy)

    def grads_of(place, out, dst, sem):
        for h in range(2):
            cols = slice(h * HALF, (h + 1) * HALF)
            value = gath[h, :, :, :, :, place * HALF:(place + 1) * HALF].reshape(TOKENS, HALF)
            out[:, cols] = dot(tok_t[...], value, ((1,), (0,))).astype(BF)
        put_out(out, dst, sem)

    grads_of(1, out_g, gg_ref, out_sem.at[0])
    op_in_send(CHUNKS - 1)
    grads_of(2, out_u, ug_ref, out_sem.at[1])
    for h in range(2):
        cols = slice(h * HALF, (h + 1) * HALF)
        out_d[cols, :] = dot(hid_t[h], grd[...].reshape(TOKENS, WIDTH), ((1,), (0,))).astype(BF)
    put_out(out_d, dg_ref, out_sem.at[2])

    total = in_own[0, core].astype(F32)
    for slot in range(1, CHIPS):
        state["iz", slot].wait_recv()
        total = total + in_far[slot].astype(F32)
    ing_ref[...] = total.astype(BF)

    for copy in started:
        copy.wait_send()
    for copy in outs:
        copy.wait()


def body(tokens, out_grad, w_gate, w_up, w_down):
    any_space = pl.BlockSpec(memory_space=pl.ANY)
    dma = pltpu.SemaphoreType.DMA
    vmem = pltpu.VMEM
    return pl.pallas_call(
        kernel,
        out_shape=(
            jax.ShapeDtypeStruct((OWN, WIDTH), BF),
            jax.ShapeDtypeStruct((WIDTH, HID), BF),
            jax.ShapeDtypeStruct((WIDTH, HID), BF),
            jax.ShapeDtypeStruct((HID, WIDTH), BF),
        ),
        in_specs=[any_space] * 5,
        out_specs=(pl.BlockSpec(memory_space=pltpu.VMEM), any_space, any_space, any_space),
        scratch_shapes=[
            vmem((CHIPS, CORES, OWN, WIDTH), BF),
            vmem((CHIPS, CORES, OWN, WIDTH), BF),
            vmem((WIDTH, TOKENS), BF),
            vmem((2, HALF, TOKENS), BF),
            vmem((WIDTH, HID), BF),
            vmem((WIDTH, HID), BF),
            vmem((HID, WIDTH), BF),
            vmem((CHUNKS, 2, RING, RING, SUB, CAT), BF),
            vmem((2, CHUNKS, RING, RING, SUB, CAT), BF),
            vmem((CHUNKS, 2, RING, SUB, CAT), BF),
            vmem((CHUNKS, 2, 2, RING, SUB, CAT), BF),
            vmem((CHUNKS, 2, SUB, CAT), BF),
            vmem((CHUNKS, 2, 2, SUB, CAT), BF),
            vmem((CHIPS, CORES, OWN, WIDTH), BF),
            vmem((CHIPS, OWN, WIDTH), BF),
            vmem((CHIPS, OWN, WIDTH), BF),
            vmem((WIDTH, HID), BF),
            vmem((WIDTH, HID), BF),
            vmem((HID, WIDTH), BF),
            dma((5,)), dma((CHIPS, 2)), dma((CHIPS, 2)), dma((CHIPS, 2)), dma((CHIPS, 2)),
            dma((CHUNKS, 24)), dma((CHUNKS, 24)), dma((CHUNKS,)), dma((CHUNKS,)),
            dma((CHIPS,)), dma((CHIPS,)), dma((3,)),
        ],
        compiler_params=pltpu.CompilerParams(
            collective_id=0, has_side_effects=True, vmem_limit_bytes=60 * 2**20),
        cost_estimate=pl.CostEstimate(
            flops=16 * TOKENS * WIDTH * HID, bytes_accessed=12 * WIDTH * HID, transcendentals=OWN * HID),
    )(tokens, out_grad, w_gate, w_up, w_down)


def solution(mesh):
    placed = (P("col", "row"), P("col", "row"), P("row", "col"), P("row", "col"), P("col", "row"))
    return jax.shard_map(
        body,
        mesh=mesh,
        in_specs=placed,
        out_specs=(P("col", "row"), P("row", "col"), P("row", "col"), P("col", "row")),
        check_vma=False,
    )
```

```python
import functools

import jax
import jax.numpy as jnp
from jax import lax
from jax.experimental import pallas as pl
from jax.experimental.pallas import tpu as pltpu
from jax.sharding import PartitionSpec as P

MESH = pl.DeviceIdType.MESH
BF = jnp.bfloat16
F32 = jnp.float32

RING = 4
CHIPS = 8
CORES = 2
CHUNKS = 4
OWN = 64
SUB = 16
WIDTH = 512
HID = 1792
HALF = HID // 2
CAT = 3 * HALF
TOKENS = 1024

CHIP_OF = (0, 1, 2, 5, 3, 4, 6, 7)
PLACE_OF = tuple(CHIP_OF.index(step) for step in range(CHIPS))
CHIP_ROWS = CORES * OWN
RESULTS = ((OWN, WIDTH), (WIDTH, HID), (WIDTH, HID), (HID, WIDTH))

ORDER = (
    ("first", 0), ("zf2", 9), ("far4", 9), ("rs_a1", 0), ("fwd1", 1), ("part", 1), ("zf3", 9), ("far67", 9),
    ("rs_a2", 0), ("fwd2", 2), ("rs_a1", 1), ("rs_b1", 0), ("part", 2), ("rs_a2", 1), ("rs_a1", 2), ("fwd3", 3),
    ("part", 3), ("rs_a2", 2), ("rs_a1", 3), ("rs_b2", 0), ("rs_b1", 1), ("rs_b1", 2), ("ag_b1", 0), ("rs_a2", 3),
    ("rs_b2", 2), ("rs_b2", 1), ("rs_b1", 3), ("ag_b1", 2), ("ag_b2", 0), ("rs_b2", 3), ("ag_b2", 2), ("ag_b1", 3),
    ("ag_a1", 2), ("ag_b1", 1), ("ag_b2", 3), ("ag_a1", 3), ("ag_b2", 1), ("ag_a2", 3), ("ag_a2", 2), ("in_part", 2),
    ("in_part", 3), ("ag_a1", 1), ("in_send", 3), ("ag_a1", 0), ("in_send", 2), ("acc_g", 0), ("acc_g", 1),
    ("acc_u", 0), ("acc_u", 1), ("ag_a2", 1), ("in_part", 1), ("acc_d", 0), ("acc_d", 1), ("in_send", 1),
    ("ag_a2", 0),
)


def dot(left, right, dims):
    return lax.dot_general(left, right, (dims, ((), ())), preferred_element_type=F32)


def kernel(
    tok_in, grd_in, wg_in, wu_in, wd_in, ing_ref, out_g, out_u, out_d,
    tok, grd, tok_t, hid_t, wg, wu, wd, part, gath, relay_a, land_a, relay_b, land_b,
    in_own, in_sib, in_far,
    load_sem, z_send, z_recv, f_send, f_recv, send, recv, i_send, i_recv, j_send, j_recv,
):
    row, col = lax.axis_index("row"), lax.axis_index("col")
    x, y = row % RING, row // RING
    z, core = col // CORES, col % CORES
    pa, pb = x + core * (y - x), y + core * (x - y)
    step_a, step_b = 1 + 3 * core, RING - 3 * core

    def at(a, b):
        return (a * step_a + b * step_b, col)

    up_a, down_a, opp_a = (pa + 1) % RING, (pa + 3) % RING, (pa + 2) % RING
    up_b, down_b, opp_b = (pb + 1) % RING, (pb + 3) % RING, (pb + 2) % RING
    dev_up_a, dev_down_a = at(up_a, pb), at(down_a, pb)
    dev_up_b, dev_down_b = at(pa, up_b), at(pa, down_b)
    sibling = (row, z * CORES + 1 - core)

    def far(step):
        return (row, ((z + step) % CHIPS) * CORES + core)

    loads = [
        pltpu.make_async_copy(tok_in, tok.at[0, core], load_sem.at[0]),
        pltpu.make_async_copy(grd_in, grd.at[0, core], load_sem.at[1]),
        pltpu.make_async_copy(wg_in, wg, load_sem.at[2]),
        pltpu.make_async_copy(wu_in, wu, load_sem.at[3]),
        pltpu.make_async_copy(wd_in, wd, load_sem.at[4]),
    ]
    for copy in loads:
        copy.start()

    barrier = pltpu.get_barrier_semaphore()
    peers = [dev_up_a, dev_down_a, dev_up_b, dev_down_b, sibling] + [far(s) for s in range(1, CHIPS)]
    for peer in peers:
        pl.semaphore_signal(barrier, inc=1, device_id=peer, device_id_type=MESH)
    pl.semaphore_wait(barrier, len(peers))

    started = []

    def push(src, dst, send_sem, recv_sem, device):
        copy = pltpu.make_async_remote_copy(
            src_ref=src, dst_ref=dst, send_sem=send_sem, recv_sem=recv_sem,
            device_id=device, device_id_type=MESH,
        )
        copy.start()
        started.append(copy)
        return copy

    from_sib, from_far = {}, {}

    def to_sibling(slot, src_tok, src_grd):
        from_sib[slot] = [
            push(src_tok, tok.at[slot, core], f_send.at[slot, 0], f_recv.at[slot, 0], sibling),
            push(src_grd, grd.at[slot, core], f_send.at[slot, 1], f_recv.at[slot, 1], sibling),
        ]

    def to_far(step):
        slot, device = PLACE_OF[step], far(CHIPS - step)
        from_far[slot] = [
            push(tok_in, tok.at[slot, core], z_send.at[slot, 0], z_recv.at[slot, 0], device),
            push(grd_in, grd.at[slot, core], z_send.at[slot, 1], z_recv.at[slot, 1], device),
        ]

    def relay_far(step):
        place, after = PLACE_OF[step], PLACE_OF[step + 1]
        from_far[after] = [
            push(tok.at[place, core], tok.at[after, core], z_send.at[after, 0], z_recv.at[after, 0], far(CHIPS - 1)),
            push(grd.at[place, core], grd.at[after, core], z_send.at[after, 1], z_recv.at[after, 1], far(CHIPS - 1)),
        ]

    def forward(slot):
        for copy in from_far[slot]:
            copy.wait_recv()
        to_sibling(slot, tok.at[slot, core], grd.at[slot, core])

    to_far(1)
    to_sibling(0, tok_in, grd_in)
    to_far(5)

    def settle(slot):
        for copy in from_sib[slot]:
            copy.wait_recv()

    def partial(j, first, count, ready=lambda i: None):
        slot, rows = 2 * j + first, count * CHIP_ROWS
        tokens = tok[slot:slot + count].reshape(rows, WIDTH)
        grads = grd[slot:slot + count].reshape(rows, WIDTH)
        for h in range(2):
            cols = slice(h * HALF, (h + 1) * HALF)

            def put(place, value):
                value = value.astype(BF)
                for i in range(count):
                    sub = 2 * (first + i)
                    part[j, h, :, sub:sub + 2, :, place * HALF:(place + 1) * HALF] = (
                        value[i * CHIP_ROWS:(i + 1) * CHIP_ROWS].reshape(RING, 2, SUB, HALF))

            if h == 0:
                ready(0)
            put(0, dot(tokens, wg[:, cols], ((1,), (0,))))
            if h == 0:
                ready(1)
            put(1, dot(tokens, wu[:, cols], ((1,), (0,))))
            if h == 0:
                ready(2)
            put(2, dot(grads, wd[cols, :], ((1,), (1,))))

    def turn(j):
        chips = [tok[2 * j + i].reshape(CHIP_ROWS, WIDTH) for i in range(2)]
        rows = [chips[i][32 * b:32 * b + 32] for b in range(RING) for i in range(2)]
        tok_t[:, j * 256:(j + 1) * 256] = jnp.concatenate(rows, axis=0).T

    def scatter_start(j, base, view, relay, land, me_up, me_down, me_opp, to_up, to_down):
        return {
            "r0": [push(view(0, me_opp), relay(0), send.at[j, base], recv.at[j, base], to_up)],
            "r1": [push(view(1, me_opp), relay(1), send.at[j, base + 1], recv.at[j, base + 1], to_down)],
            "u1": [push(view(1, me_up), land(0, 1), send.at[j, base + 2], recv.at[j, base + 2], to_up)],
            "d0": [push(view(0, me_down), land(1, 0), send.at[j, base + 3], recv.at[j, base + 3], to_down)],
        }

    def settle_all(copies, *names):
        for name in names:
            for copy in copies[name]:
                copy.wait_recv()

    def scatter_relay(j, base, copies, view, add, land, me_up, me_down, to_up, to_down):
        settle_all(copies, "r0")
        add(0, me_up)
        copies["u0"] = [push(view(0, me_up), land(0, 0), send.at[j, base + 4], recv.at[j, base + 4], to_up)]
        settle_all(copies, "r1")
        add(1, me_down)
        copies["d1"] = [push(view(1, me_down), land(1, 1), send.at[j, base + 5], recv.at[j, base + 5], to_down)]

    def settle_scatter(copies):
        settle_all(copies, "u1", "d0", "u0", "d1")

    def gather_start(j, base, view, to_up, to_down):
        return {
            "u0": push(view(0), view(0), send.at[j, base], recv.at[j, base], to_up),
            "d1": push(view(1), view(1), send.at[j, base + 1], recv.at[j, base + 1], to_down),
            "u1": push(view(1), view(1), send.at[j, base + 2], recv.at[j, base + 2], to_up),
            "d0": push(view(0), view(0), send.at[j, base + 3], recv.at[j, base + 3], to_down),
        }

    def gather_relay(j, base, copies, view_down, view_up, to_up, to_down):
        copies["u0"].wait_recv()
        copies["f0"] = push(view_down(0), view_down(0), send.at[j, base + 4], recv.at[j, base + 4], to_up)
        copies["d1"].wait_recv()
        copies["f1"] = push(view_up(1), view_up(1), send.at[j, base + 5], recv.at[j, base + 5], to_down)

    def settle_gather(copies):
        for name in ("u1", "d0", "f0", "f1"):
            copies[name].wait_recv()

    state = {}

    def view_a(j):
        return lambda h, block: part.at[j, h, block]

    def view_b(j):
        return lambda h, block: part.at[j, h, pa, block]

    def land_view(land, j):
        return lambda side, h: land.at[j, side, h]

    def relay_view(relay, j):
        return lambda h: relay.at[j, h]

    def begin(j):
        state["ra", j] = scatter_start(
            j, 0, view_a(j), relay_view(relay_a, j), land_view(land_a, j), up_a, down_a, opp_a, dev_up_a, dev_down_a)

    def begin_half(j, i):
        subs = slice(2 * i, 2 * i + 2)
        copies = scatter_start(
            j, 24 if i else 0, lambda h, block: part.at[j, h, block, subs], lambda h: relay_a.at[j, h, subs],
            lambda side, h: land_a.at[j, side, h, subs], up_a, down_a, opp_a, dev_up_a, dev_down_a)
        if i:
            copies = {name: state["ra", j][name] + copies[name] for name in copies}
        state["ra", j] = copies

    def op_first(j):
        loads[0].wait()
        loads[1].wait()
        settle(0)
        partial(0, 0, 1, lambda i: loads[2 + i].wait())
        begin_half(0, 0)
        forward(1)
        relay_far(1)
        settle(1)
        partial(0, 1, 1)
        begin_half(0, 1)
        turn(0)

    def op_zf2(j):
        forward(PLACE_OF[2])
        relay_far(2)

    def op_far4(j):
        to_far(4)

    def op_zf3(j):
        forward(PLACE_OF[3])

    def op_far67(j):
        to_far(6)
        to_far(7)

    def op_fwd1(j):
        forward(PLACE_OF[5])

    def op_fwd2(j):
        forward(PLACE_OF[4])

    def op_fwd3(j):
        forward(PLACE_OF[7])
        forward(PLACE_OF[6])

    def op_part(j):
        settle(2 * j)
        settle(2 * j + 1)
        partial(j, 0, 2)
        begin(j)
        turn(j)

    def op_rs_a1(j):
        def add(h, block):
            def some(i, carry):
                total = part[j, h, block, i].astype(F32) + relay_a[j, h, i].astype(F32)
                part[j, h, block, i] = total.astype(BF)
                return carry
            lax.fori_loop(0, RING, some, 0)
        scatter_relay(
            j, 0, state["ra", j], view_a(j), add, land_view(land_a, j), up_a, down_a, dev_up_a, dev_down_a)

    def op_rs_a2(j):
        settle_scatter(state["ra", j])
        for h in range(2):
            def some(i, carry):
                total = part[j, h, pa, i].astype(F32) + land_a[j, 0, h, i].astype(F32)
                part[j, h, pa, i] = (total + land_a[j, 1, h, i].astype(F32)).astype(BF)
                return carry
            lax.fori_loop(0, RING, some, 0)
        state["rb", j] = scatter_start(
            j, 6, view_b(j), relay_view(relay_b, j), land_view(land_b, j), up_b, down_b, opp_b, dev_up_b, dev_down_b)

    def op_rs_b1(j):
        def add(h, block):
            total = part[j, h, pa, block].astype(F32) + relay_b[j, h].astype(F32)
            part[j, h, pa, block] = total.astype(BF)
        scatter_relay(
            j, 6, state["rb", j], view_b(j), add, land_view(land_b, j), up_b, down_b, dev_up_b, dev_down_b)

    def op_rs_b2(j):
        settle_scatter(state["rb", j])
        for h in range(2):
            def total(place):
                cols = slice(place * HALF, (place + 1) * HALF)
                value = part[j, h, pa, pb, :, cols].astype(F32) + land_b[j, 0, h, :, cols].astype(F32)
                value = value + land_b[j, 1, h, :, cols].astype(F32)
                return value.astype(BF).astype(F32)
            g_val, u_val, d_val = total(0), total(1), total(2)
            sig = 1.0 / (1.0 + jnp.exp(-g_val))
            act = g_val * sig
            gath[h, j, pa, pb, :, 0:HALF] = (act * u_val).astype(BF)
            gath[h, j, pa, pb, :, HALF:2 * HALF] = (d_val * u_val * sig * (1.0 + g_val * (1.0 - sig))).astype(BF)
            gath[h, j, pa, pb, :, 2 * HALF:] = (d_val * act).astype(BF)
        state["gb", j] = gather_start(j, 12, lambda h: gath.at[h, j, pa, pb], dev_up_b, dev_down_b)

    def op_ag_b1(j):
        gather_relay(
            j, 12, state["gb", j], lambda h: gath.at[h, j, pa, down_b], lambda h: gath.at[h, j, pa, up_b],
            dev_up_b, dev_down_b)

    def op_ag_b2(j):
        settle_gather(state["gb", j])
        state["ga", j] = gather_start(j, 18, lambda h: gath.at[h, j, pa], dev_up_a, dev_down_a)

    def op_ag_a1(j):
        gather_relay(
            j, 18, state["ga", j], lambda h: gath.at[h, j, down_a], lambda h: gath.at[h, j, up_a],
            dev_up_a, dev_down_a)

    def op_ag_a2(j):
        settle_gather(state["ga", j])

    def gathered(h, j, place):
        cols = slice(place * HALF, (place + 1) * HALF)
        chips = [gath[h, j, :, 2 * i:2 * i + 2, :, cols].reshape(CHIP_ROWS, HALF) for i in range(2)]
        return jnp.concatenate(chips, axis=0)

    def in_half(j, i):
        total = None
        for h in range(2):
            cols = slice(h * HALF, (h + 1) * HALF)
            for place, weight in ((1, wg), (2, wu)):
                value = gath[h, j, :, 2 * i:2 * i + 2, :, place * HALF:(place + 1) * HALF].reshape(CHIP_ROWS, HALF)
                term = dot(value, weight[:, cols], ((1,), (1,)))
                total = term if total is None else total + term
        slot = 2 * j + i
        in_own[slot] = total.astype(BF).reshape(CORES, OWN, WIDTH)
        sem = j if i else CHUNKS
        return push(in_own.at[slot, 1 - core], in_sib.at[slot], i_send.at[sem], i_recv.at[sem], sibling)

    def pair(slot):
        value = in_own[slot, core].astype(F32) + in_sib[slot].astype(F32)
        in_own[slot, core] = value.astype(BF)
        if slot:
            state["iz", slot] = push(
                in_own.at[slot, core], in_far.at[slot], j_send.at[slot], j_recv.at[slot], far(CHIP_OF[slot]))

    def turn_hidden(j):
        for h in range(2):
            hid_t[h, :, j * 256:(j + 1) * 256] = gathered(h, j, 0).T

    def op_in_part(j):
        total = None
        for h in range(2):
            cols = slice(h * HALF, (h + 1) * HALF)
            for place, weight in ((1, wg), (2, wu)):
                term = dot(gathered(h, j, place), weight[:, cols], ((1,), (1,)))
                total = term if total is None else total + term
        in_own[2 * j:2 * j + 2] = total.astype(BF).reshape(2, CORES, OWN, WIDTH)
        state["is", j] = push(
            in_own.at[2 * j:2 * j + 2, 1 - core], in_sib.at[2 * j:2 * j + 2], i_send.at[j], i_recv.at[j], sibling)
        turn_hidden(j)

    def op_in_send(j):
        state["is", j].wait_recv()
        for slot in sorted((2 * j, 2 * j + 1), key=lambda p: -min(CHIP_OF[p], CHIPS - CHIP_OF[p])):
            pair(slot)

    def grads_of(h, place, j, count, out, more=False):
        cols = slice(h * HALF, (h + 1) * HALF)
        rows = slice(j * 256, (j + count) * 256)
        value = gath[h, j:j + count, :, :, :, place * HALF:(place + 1) * HALF].reshape(count * 256, HALF)
        term = dot(tok_t[:, rows], value, ((1,), (0,)))
        if more:
            term = out[:, cols].astype(F32) + term
        out[:, cols] = term.astype(BF)

    def down_of(h, j, count, more=False):
        cols = slice(h * HALF, (h + 1) * HALF)
        rows = slice(j * 256, (j + count) * 256)
        grads = grd[2 * j:2 * (j + count)].reshape(count * 256, WIDTH)
        term = dot(hid_t[h, :, rows], grads, ((1,), (0,)))
        if more:
            term = out_d[cols, :].astype(F32) + term
        out_d[cols, :] = term.astype(BF)

    def op_acc_g(h):
        grads_of(h, 1, 2, 2, out_g)

    def op_acc_u(h):
        grads_of(h, 2, 2, 2, out_u)

    def op_acc_d(h):
        down_of(h, 2, 2)

    ops = dict(
        acc_g=op_acc_g, acc_u=op_acc_u, acc_d=op_acc_d,
        first=op_first, zf2=op_zf2, zf3=op_zf3, far4=op_far4, far67=op_far67, fwd1=op_fwd1, fwd2=op_fwd2, fwd3=op_fwd3,
        part=op_part, rs_a1=op_rs_a1, rs_a2=op_rs_a2, rs_b1=op_rs_b1, rs_b2=op_rs_b2,
        ag_b1=op_ag_b1, ag_b2=op_ag_b2, ag_a1=op_ag_a1, ag_a2=op_ag_a2, in_part=op_in_part, in_send=op_in_send,
    )
    for name, j in ORDER:
        ops[name](j)

    near = in_half(0, 1)
    own = in_half(0, 0)
    near.wait_recv()
    pair(1)
    for h in range(2):
        grads_of(h, 1, 0, 2, out_g, True)
    turn_hidden(0)
    own.wait_recv()
    pair(0)
    for h in range(2):
        grads_of(h, 2, 0, 2, out_u, True)
    for h in range(2):
        down_of(h, 0, 2, True)

    total = in_own[0, core].astype(F32)
    for slot in range(1, CHIPS):
        state["iz", slot].wait_recv()
        total = total + in_far[slot].astype(F32)
    ing_ref[...] = total.astype(BF)

    for copy in started:
        copy.wait_send()


def store(*refs):
    sems = refs[-1]
    copies = [pltpu.make_async_copy(refs[i], refs[4 + i], sems.at[i]) for i in range(4)]
    for copy in copies:
        copy.start()
    for copy in copies:
        copy.wait()


def body(tokens, out_grad, w_gate, w_up, w_down):
    any_space = pl.BlockSpec(memory_space=pl.ANY)
    dma = pltpu.SemaphoreType.DMA
    vmem = pltpu.VMEM
    placed = [pltpu.with_memory_space_constraint(v, pltpu.HBM) for v in (tokens, out_grad, w_gate, w_up, w_down)]
    held = pl.pallas_call(
        kernel,
        out_shape=tuple(vmem(shape, BF) for shape in RESULTS),
        in_specs=[pl.BlockSpec(memory_space=pltpu.HBM)] * 5,
        out_specs=(pl.BlockSpec(memory_space=pltpu.VMEM),) * 4,
        scratch_shapes=[
            vmem((CHIPS, CORES, OWN, WIDTH), BF),
            vmem((CHIPS, CORES, OWN, WIDTH), BF),
            vmem((WIDTH, TOKENS), BF),
            vmem((2, HALF, TOKENS), BF),
            vmem((WIDTH, HID), BF),
            vmem((WIDTH, HID), BF),
            vmem((HID, WIDTH), BF),
            vmem((CHUNKS, 2, RING, RING, SUB, CAT), BF),
            vmem((2, CHUNKS, RING, RING, SUB, CAT), BF),
            vmem((CHUNKS, 2, RING, SUB, CAT), BF),
            vmem((CHUNKS, 2, 2, RING, SUB, CAT), BF),
            vmem((CHUNKS, 2, SUB, CAT), BF),
            vmem((CHUNKS, 2, 2, SUB, CAT), BF),
            vmem((CHIPS, CORES, OWN, WIDTH), BF),
            vmem((CHIPS, OWN, WIDTH), BF),
            vmem((CHIPS, OWN, WIDTH), BF),
            dma((5,)), dma((CHIPS, 2)), dma((CHIPS, 2)), dma((CHIPS, 2)), dma((CHIPS, 2)),
            dma((CHUNKS, 28)), dma((CHUNKS, 28)), dma((CHUNKS + 1,)), dma((CHUNKS + 1,)),
            dma((CHIPS,)), dma((CHIPS,)),
        ],
        compiler_params=pltpu.CompilerParams(
            collective_id=0, has_side_effects=True, vmem_limit_bytes=48 * 2**20),
        cost_estimate=pl.CostEstimate(
            flops=16 * TOKENS * WIDTH * HID, bytes_accessed=12 * WIDTH * HID, transcendentals=OWN * HID),
    )(*placed)
    held = [pltpu.with_memory_space_constraint(v, pltpu.VMEM) for v in held]
    return pl.pallas_call(
        store,
        out_shape=tuple(jax.ShapeDtypeStruct(shape, BF) for shape in RESULTS),
        in_specs=[any_space] * 4,
        out_specs=(any_space,) * 4,
        scratch_shapes=[dma((4,))],
        compiler_params=pltpu.CompilerParams(vmem_limit_bytes=2**20),
    )(*held)


def solution(mesh):
    placed = (P("col", "row"), P("col", "row"), P("row", "col"), P("row", "col"), P("col", "row"))
    return jax.shard_map(
        body,
        mesh=mesh,
        in_specs=placed,
        out_specs=(P("col", "row"), P("row", "col"), P("row", "col"), P("col", "row")),
        check_vma=False,
    )
```

```python
import functools

import jax
import jax.numpy as jnp
from jax import lax
from jax.experimental import pallas as pl
from jax.experimental.pallas import tpu as pltpu
from jax.sharding import PartitionSpec as P

MESH = pl.DeviceIdType.MESH
BF = jnp.bfloat16
F32 = jnp.float32

RING = 4
CHIPS = 8
CORES = 2
CHUNKS = 4
OWN = 64
SUB = 16
WIDTH = 512
HID = 1792
HALF = HID // 2
CAT = 3 * HALF
TOKENS = 1024

CHIP_OF = (0, 1, 2, 5, 3, 4, 6, 7)
PLACE_OF = tuple(CHIP_OF.index(step) for step in range(CHIPS))
CHIP_ROWS = CORES * OWN
LAST = 0
HIDDEN, GRADS = slice(0, HALF), slice(HALF, CAT)
RESULTS = ((OWN, WIDTH), (WIDTH, HID), (WIDTH, HID), (HID, WIDTH))

ORDER = (
    ("first", 0), ("zf2", 9), ("rs_a1", 0), ("fwd1", 1), ("far4", 9), ("part", 1), ("zf3", 9), ("rs_a2", 0),
    ("far67", 9), ("rs_a1", 1), ("rs_b1", 0), ("fwd2", 2), ("part", 2), ("fwd3", 3), ("part", 3), ("rs_a2", 1),
    ("rs_b2", 0), ("rs_b1", 1), ("rs_a1", 3), ("rs_b2", 1), ("rs_a1", 2), ("ag_b1", 1), ("rs_a2", 3), ("ag_b2", 1),
    ("rs_b1", 3), ("rs_a2", 2), ("rs_b2", 3), ("ag_a1", 1), ("rs_b1", 2), ("ag_b1", 3), ("rs_b2", 2), ("ag_b2", 3),
    ("ag_b1", 0), ("ag_b1", 2), ("ag_a1", 3), ("ag_b2", 2), ("ag_a2", 1), ("in_part", 1), ("in_send", 1),
    ("ag_a1", 2), ("ag_a2", 3), ("ag_b2", 0), ("in_part", 3), ("ag_a2", 2), ("in_send", 3), ("in_part", 2),
    ("acc_g", 0), ("ag_a1", 0), ("in_send", 2), ("acc_u", 0), ("acc_u", 1), ("acc_g", 1), ("acc_d", 1), ("acc_d", 0),
    ("drain", 8), ("ag_a2", 0),
)


def dot(left, right, dims):
    return lax.dot_general(left, right, (dims, ((), ())), preferred_element_type=F32)


def kernel(
    tok_in, grd_in, wg_in, wu_in, wd_in, ing_ref, out_g, out_u, out_d,
    tok, grd, tok_t, hid_t, wg, wu, wd, part, gath, relay_a, land_a, relay_b, land_b,
    in_own, in_sib, in_far,
    load_sem, z_send, z_recv, f_send, f_recv, send, recv, i_send, i_recv, j_send, j_recv,
):
    row, col = lax.axis_index("row"), lax.axis_index("col")
    x, y = row % RING, row // RING
    z, core = col // CORES, col % CORES
    pa, pb = x + core * (y - x), y + core * (x - y)
    step_a, step_b = 1 + 3 * core, RING - 3 * core

    def at(a, b):
        return (a * step_a + b * step_b, col)

    up_a, down_a, opp_a = (pa + 1) % RING, (pa + 3) % RING, (pa + 2) % RING
    up_b, down_b, opp_b = (pb + 1) % RING, (pb + 3) % RING, (pb + 2) % RING
    dev_up_a, dev_down_a = at(up_a, pb), at(down_a, pb)
    dev_up_b, dev_down_b = at(pa, up_b), at(pa, down_b)
    sibling = (row, z * CORES + 1 - core)

    def far(step):
        return (row, ((z + step) % CHIPS) * CORES + core)

    loads = [
        pltpu.make_async_copy(tok_in, tok.at[0, core], load_sem.at[0]),
        pltpu.make_async_copy(grd_in, grd.at[0, core], load_sem.at[1]),
        pltpu.make_async_copy(wg_in, wg, load_sem.at[2]),
        pltpu.make_async_copy(wu_in, wu, load_sem.at[3]),
        pltpu.make_async_copy(wd_in, wd, load_sem.at[4]),
    ]
    for copy in loads:
        copy.start()

    barrier = pltpu.get_barrier_semaphore()
    peers = [dev_up_a, dev_down_a, dev_up_b, dev_down_b, sibling] + [far(s) for s in range(1, CHIPS)]
    for peer in peers:
        pl.semaphore_signal(barrier, inc=1, device_id=peer, device_id_type=MESH)
    pl.semaphore_wait(barrier, len(peers))

    started = []

    def push(src, dst, send_sem, recv_sem, device):
        copy = pltpu.make_async_remote_copy(
            src_ref=src, dst_ref=dst, send_sem=send_sem, recv_sem=recv_sem,
            device_id=device, device_id_type=MESH,
        )
        copy.start()
        started.append(copy)
        return copy

    from_sib, from_far = {}, {}

    def to_sibling(slot, src_tok, src_grd):
        from_sib[slot] = [
            push(src_tok, tok.at[slot, core], f_send.at[slot, 0], f_recv.at[slot, 0], sibling),
            push(src_grd, grd.at[slot, core], f_send.at[slot, 1], f_recv.at[slot, 1], sibling),
        ]

    def to_far(step):
        slot, device = PLACE_OF[step], far(CHIPS - step)
        from_far[slot] = [
            push(tok_in, tok.at[slot, core], z_send.at[slot, 0], z_recv.at[slot, 0], device),
            push(grd_in, grd.at[slot, core], z_send.at[slot, 1], z_recv.at[slot, 1], device),
        ]

    def relay_far(step):
        place, after = PLACE_OF[step], PLACE_OF[step + 1]
        from_far[after] = [
            push(tok.at[place, core], tok.at[after, core], z_send.at[after, 0], z_recv.at[after, 0], far(CHIPS - 1)),
            push(grd.at[place, core], grd.at[after, core], z_send.at[after, 1], z_recv.at[after, 1], far(CHIPS - 1)),
        ]

    def forward(slot):
        for copy in from_far[slot]:
            copy.wait_recv()
        to_sibling(slot, tok.at[slot, core], grd.at[slot, core])

    to_far(1)
    to_sibling(0, tok_in, grd_in)
    to_far(5)

    def settle(slot):
        for copy in from_sib[slot]:
            copy.wait_recv()

    def partial(j, first, count, ready=lambda i: None):
        slot, rows = 2 * j + first, count * CHIP_ROWS
        tokens = tok[slot:slot + count].reshape(rows, WIDTH)
        grads = grd[slot:slot + count].reshape(rows, WIDTH)
        for h in range(2):
            cols = slice(h * HALF, (h + 1) * HALF)

            def put(place, value):
                value = value.astype(BF)
                for i in range(count):
                    sub = 2 * (first + i)
                    part[j, h, :, sub:sub + 2, :, place * HALF:(place + 1) * HALF] = (
                        value[i * CHIP_ROWS:(i + 1) * CHIP_ROWS].reshape(RING, 2, SUB, HALF))

            if h == 0:
                ready(0)
            put(0, dot(tokens, wg[:, cols], ((1,), (0,))))
            if h == 0:
                ready(1)
            put(1, dot(tokens, wu[:, cols], ((1,), (0,))))
            if h == 0:
                ready(2)
            put(2, dot(grads, wd[cols, :], ((1,), (1,))))

    def turn(j):
        chips = [tok[2 * j + i].reshape(CHIP_ROWS, WIDTH) for i in range(2)]
        rows = [chips[i][32 * b:32 * b + 32] for b in range(RING) for i in range(2)]
        tok_t[:, j * 256:(j + 1) * 256] = jnp.concatenate(rows, axis=0).T

    def scatter_start(j, base, view, relay, land, me_up, me_down, me_opp, to_up, to_down):
        return {
            "r0": [push(view(0, me_opp), relay(0), send.at[j, base], recv.at[j, base], to_up)],
            "r1": [push(view(1, me_opp), relay(1), send.at[j, base + 1], recv.at[j, base + 1], to_down)],
            "u1": [push(view(1, me_up), land(0, 1), send.at[j, base + 2], recv.at[j, base + 2], to_up)],
            "d0": [push(view(0, me_down), land(1, 0), send.at[j, base + 3], recv.at[j, base + 3], to_down)],
        }

    def settle_all(copies, *names):
        for name in names:
            for copy in copies[name]:
                copy.wait_recv()

    def scatter_relay(j, base, copies, view, add, land, me_up, me_down, to_up, to_down):
        settle_all(copies, "r0")
        add(0, me_up)
        copies["u0"] = [push(view(0, me_up), land(0, 0), send.at[j, base + 4], recv.at[j, base + 4], to_up)]
        settle_all(copies, "r1")
        add(1, me_down)
        copies["d1"] = [push(view(1, me_down), land(1, 1), send.at[j, base + 5], recv.at[j, base + 5], to_down)]

    def settle_scatter(copies):
        settle_all(copies, "u1", "d0", "u0", "d1")

    def gather_start(j, base, view, to_up, to_down):
        return {
            "u0": push(view(0), view(0), send.at[j, base], recv.at[j, base], to_up),
            "d1": push(view(1), view(1), send.at[j, base + 1], recv.at[j, base + 1], to_down),
            "u1": push(view(1), view(1), send.at[j, base + 2], recv.at[j, base + 2], to_up),
            "d0": push(view(0), view(0), send.at[j, base + 3], recv.at[j, base + 3], to_down),
        }

    def gather_relay(j, base, copies, view_down, view_up, to_up, to_down):
        copies["u0"].wait_recv()
        copies["f0"] = push(view_down(0), view_down(0), send.at[j, base + 4], recv.at[j, base + 4], to_up)
        copies["d1"].wait_recv()
        copies["f1"] = push(view_up(1), view_up(1), send.at[j, base + 5], recv.at[j, base + 5], to_down)

    def settle_gather(copies):
        for name in ("u1", "d0", "f0", "f1"):
            copies[name].wait_recv()

    state = {}

    def view_a(j):
        return lambda h, block: part.at[j, h, block]

    def view_b(j):
        return lambda h, block: part.at[j, h, pa, block]

    def land_view(land, j):
        return lambda side, h: land.at[j, side, h]

    def relay_view(relay, j):
        return lambda h: relay.at[j, h]

    def begin(j):
        state["ra", j] = scatter_start(
            j, 0, view_a(j), relay_view(relay_a, j), land_view(land_a, j), up_a, down_a, opp_a, dev_up_a, dev_down_a)

    def begin_half(j, i):
        subs = slice(2 * i, 2 * i + 2)
        copies = scatter_start(
            j, 24 if i else 0, lambda h, block: part.at[j, h, block, subs], lambda h: relay_a.at[j, h, subs],
            lambda side, h: land_a.at[j, side, h, subs], up_a, down_a, opp_a, dev_up_a, dev_down_a)
        if i:
            copies = {name: state["ra", j][name] + copies[name] for name in copies}
        state["ra", j] = copies

    def op_first(j):
        loads[0].wait()
        loads[1].wait()
        settle(0)
        partial(0, 0, 1, lambda i: loads[2 + i].wait())
        begin_half(0, 0)
        forward(1)
        relay_far(1)
        settle(1)
        partial(0, 1, 1)
        begin_half(0, 1)
        turn(0)

    def op_zf2(j):
        forward(PLACE_OF[2])
        relay_far(2)

    def op_far4(j):
        to_far(4)

    def op_zf3(j):
        forward(PLACE_OF[3])

    def op_far67(j):
        to_far(6)
        to_far(7)

    def op_fwd1(j):
        forward(PLACE_OF[5])

    def op_fwd2(j):
        forward(PLACE_OF[4])

    def op_fwd3(j):
        forward(PLACE_OF[7])
        forward(PLACE_OF[6])

    def op_part(j):
        settle(2 * j)
        settle(2 * j + 1)
        partial(j, 0, 2)
        begin(j)
        turn(j)

    def op_rs_a1(j):
        def add(h, block):
            def some(i, carry):
                total = part[j, h, block, i].astype(F32) + relay_a[j, h, i].astype(F32)
                part[j, h, block, i] = total.astype(BF)
                return carry
            lax.fori_loop(0, RING, some, 0)
        scatter_relay(
            j, 0, state["ra", j], view_a(j), add, land_view(land_a, j), up_a, down_a, dev_up_a, dev_down_a)

    def op_rs_a2(j):
        settle_scatter(state["ra", j])
        for h in range(2):
            def some(i, carry):
                total = part[j, h, pa, i].astype(F32) + land_a[j, 0, h, i].astype(F32)
                part[j, h, pa, i] = (total + land_a[j, 1, h, i].astype(F32)).astype(BF)
                return carry
            lax.fori_loop(0, RING, some, 0)
        state["rb", j] = scatter_start(
            j, 6, view_b(j), relay_view(relay_b, j), land_view(land_b, j), up_b, down_b, opp_b, dev_up_b, dev_down_b)

    def op_rs_b1(j):
        def add(h, block):
            total = part[j, h, pa, block].astype(F32) + relay_b[j, h].astype(F32)
            part[j, h, pa, block] = total.astype(BF)
        scatter_relay(
            j, 6, state["rb", j], view_b(j), add, land_view(land_b, j), up_b, down_b, dev_up_b, dev_down_b)

    def op_rs_b2(j):
        settle_scatter(state["rb", j])
        for h in range(2):
            def total(place):
                cols = slice(place * HALF, (place + 1) * HALF)
                value = part[j, h, pa, pb, :, cols].astype(F32) + land_b[j, 0, h, :, cols].astype(F32)
                value = value + land_b[j, 1, h, :, cols].astype(F32)
                return value.astype(BF).astype(F32)
            g_val, u_val, d_val = total(0), total(1), total(2)
            sig = 1.0 / (1.0 + jnp.exp(-g_val))
            act = g_val * sig
            gath[h, j, pa, pb, :, 0:HALF] = (act * u_val).astype(BF)
            gath[h, j, pa, pb, :, HALF:2 * HALF] = (d_val * u_val * sig * (1.0 + g_val * (1.0 - sig))).astype(BF)
            gath[h, j, pa, pb, :, 2 * HALF:] = (d_val * act).astype(BF)
        state["gb", j] = gather_start(j, 12, lambda h: gath.at[h, j, pa, pb], dev_up_b, dev_down_b)

    def op_ag_b1(j):
        gather_relay(
            j, 12, state["gb", j], lambda h: gath.at[h, j, pa, down_b], lambda h: gath.at[h, j, pa, up_b],
            dev_up_b, dev_down_b)

    def view_last(cols):
        return lambda h, block=None: gath.at[h, LAST, pa if block is None else block, :, :, cols]

    def op_ag_b2(j):
        settle_gather(state["gb", j])
        if j == LAST:
            state["ga", j] = gather_start(j, 18, view_last(GRADS), dev_up_a, dev_down_a)
            return
        state["ga", j] = gather_start(j, 18, lambda h: gath.at[h, j, pa], dev_up_a, dev_down_a)

    def op_ag_a1(j):
        if j == LAST:
            view = view_last(GRADS)
            gather_relay(
                j, 18, state["ga", j], lambda h: view(h, down_a), lambda h: view(h, up_a), dev_up_a, dev_down_a)
            state["gh", j] = gather_start(j, 28, view_last(HIDDEN), dev_up_a, dev_down_a)
            return
        gather_relay(
            j, 18, state["ga", j], lambda h: gath.at[h, j, down_a], lambda h: gath.at[h, j, up_a],
            dev_up_a, dev_down_a)

    def op_ag_h(j):
        view = view_last(HIDDEN)
        gather_relay(
            j, 28, state["gh", j], lambda h: view(h, down_a), lambda h: view(h, up_a), dev_up_a, dev_down_a)

    def op_ag_a2(j):
        settle_gather(state["ga", j])

    def gathered(h, j, place):
        cols = slice(place * HALF, (place + 1) * HALF)
        chips = [gath[h, j, :, 2 * i:2 * i + 2, :, cols].reshape(CHIP_ROWS, HALF) for i in range(2)]
        return jnp.concatenate(chips, axis=0)

    def in_half(j, i):
        total = None
        for h in range(2):
            cols = slice(h * HALF, (h + 1) * HALF)
            for place, weight in ((1, wg), (2, wu)):
                value = gath[h, j, :, 2 * i:2 * i + 2, :, place * HALF:(place + 1) * HALF].reshape(CHIP_ROWS, HALF)
                term = dot(value, weight[:, cols], ((1,), (1,)))
                total = term if total is None else total + term
        slot = 2 * j + i
        in_own[slot] = total.astype(BF).reshape(CORES, OWN, WIDTH)
        sem = j if i else CHUNKS
        return push(in_own.at[slot, 1 - core], in_sib.at[slot], i_send.at[sem], i_recv.at[sem], sibling)

    def pair(slot):
        value = in_own[slot, core].astype(F32) + in_sib[slot].astype(F32)
        in_own[slot, core] = value.astype(BF)
        if slot:
            state["iz", slot] = push(
                in_own.at[slot, core], in_far.at[slot], j_send.at[slot], j_recv.at[slot], far(CHIP_OF[slot]))

    def turn_hidden(j):
        for h in range(2):
            hid_t[h, :, j * 256:(j + 1) * 256] = gathered(h, j, 0).T

    def op_in_part(j):
        total = None
        for h in range(2):
            cols = slice(h * HALF, (h + 1) * HALF)
            for place, weight in ((1, wg), (2, wu)):
                term = dot(gathered(h, j, place), weight[:, cols], ((1,), (1,)))
                total = term if total is None else total + term
        in_own[2 * j:2 * j + 2] = total.astype(BF).reshape(2, CORES, OWN, WIDTH)
        state["is", j] = push(
            in_own.at[2 * j:2 * j + 2, 1 - core], in_sib.at[2 * j:2 * j + 2], i_send.at[j], i_recv.at[j], sibling)
        turn_hidden(j)

    def op_in_send(j):
        state["is", j].wait_recv()
        for slot in sorted((2 * j, 2 * j + 1), key=lambda p: -min(CHIP_OF[p], CHIPS - CHIP_OF[p])):
            pair(slot)

    def grads_of(h, place, j, count, out, more=False):
        cols = slice(h * HALF, (h + 1) * HALF)
        rows = slice(j * 256, (j + count) * 256)
        value = gath[h, j:j + count, :, :, :, place * HALF:(place + 1) * HALF].reshape(count * 256, HALF)
        term = dot(tok_t[:, rows], value, ((1,), (0,)))
        if more:
            term = out[:, cols].astype(F32) + term
        out[:, cols] = term.astype(BF)

    def down_of(h, j, count, more=False):
        cols = slice(h * HALF, (h + 1) * HALF)
        rows = slice(j * 256, (j + count) * 256)
        grads = grd[2 * j:2 * (j + count)].reshape(count * 256, WIDTH)
        term = dot(hid_t[h, :, rows], grads, ((1,), (0,)))
        if more:
            term = out_d[cols, :].astype(F32) + term
        out_d[cols, :] = term.astype(BF)

    waited = []

    def op_drain(count):
        for copy in started[len(waited):len(started) - count]:
            copy.wait_send()
            waited.append(copy)

    def op_acc_g(h):
        grads_of(h, 1, 2, 2, out_g)

    def op_acc_u(h):
        grads_of(h, 2, 2, 2, out_u)

    def op_acc_d(h):
        down_of(h, 2, 2)

    ops = dict(
        acc_g=op_acc_g, acc_u=op_acc_u, acc_d=op_acc_d, drain=op_drain,
        first=op_first, zf2=op_zf2, zf3=op_zf3, far4=op_far4, far67=op_far67, fwd1=op_fwd1, fwd2=op_fwd2, fwd3=op_fwd3,
        part=op_part, rs_a1=op_rs_a1, rs_a2=op_rs_a2, rs_b1=op_rs_b1, rs_b2=op_rs_b2,
        ag_b1=op_ag_b1, ag_b2=op_ag_b2, ag_a1=op_ag_a1, ag_a2=op_ag_a2, in_part=op_in_part, in_send=op_in_send,
    )
    for name, j in ORDER:
        ops[name](j)

    near = in_half(LAST, 1)
    op_ag_h(LAST)
    own = in_half(LAST, 0)
    near.wait_recv()
    pair(1)
    for h in range(2):
        grads_of(h, 1, 0, 2, out_g, True)
    for h in range(2):
        grads_of(h, 2, 0, 2, out_u, True)
    own.wait_recv()
    pair(0)
    settle_gather(state["gh", LAST])
    turn_hidden(LAST)
    for h in range(2):
        down_of(h, 0, 2, True)

    total = in_own[0, core].astype(F32)
    for slot in range(1, CHIPS):
        state["iz", slot].wait_recv()
        total = total + in_far[slot].astype(F32)
    ing_ref[...] = total.astype(BF)

    op_drain(0)


def store(*refs):
    sems = refs[-1]
    copies = [pltpu.make_async_copy(refs[i], refs[4 + i], sems.at[i]) for i in range(4)]
    for copy in copies:
        copy.start()
    for copy in copies:
        copy.wait()


def body(tokens, out_grad, w_gate, w_up, w_down):
    any_space = pl.BlockSpec(memory_space=pl.ANY)
    dma = pltpu.SemaphoreType.DMA
    vmem = pltpu.VMEM
    placed = [pltpu.with_memory_space_constraint(v, pltpu.HBM) for v in (tokens, out_grad, w_gate, w_up, w_down)]
    held = pl.pallas_call(
        kernel,
        out_shape=tuple(vmem(shape, BF) for shape in RESULTS),
        in_specs=[pl.BlockSpec(memory_space=pltpu.HBM)] * 5,
        out_specs=(pl.BlockSpec(memory_space=pltpu.VMEM),) * 4,
        scratch_shapes=[
            vmem((CHIPS, CORES, OWN, WIDTH), BF),
            vmem((CHIPS, CORES, OWN, WIDTH), BF),
            vmem((WIDTH, TOKENS), BF),
            vmem((2, HALF, TOKENS), BF),
            vmem((WIDTH, HID), BF),
            vmem((WIDTH, HID), BF),
            vmem((HID, WIDTH), BF),
            vmem((CHUNKS, 2, RING, RING, SUB, CAT), BF),
            vmem((2, CHUNKS, RING, RING, SUB, CAT), BF),
            vmem((CHUNKS, 2, RING, SUB, CAT), BF),
            vmem((CHUNKS, 2, 2, RING, SUB, CAT), BF),
            vmem((CHUNKS, 2, SUB, CAT), BF),
            vmem((CHUNKS, 2, 2, SUB, CAT), BF),
            vmem((CHIPS, CORES, OWN, WIDTH), BF),
            vmem((CHIPS, OWN, WIDTH), BF),
            vmem((CHIPS, OWN, WIDTH), BF),
            dma((5,)), dma((CHIPS, 2)), dma((CHIPS, 2)), dma((CHIPS, 2)), dma((CHIPS, 2)),
            dma((CHUNKS, 34)), dma((CHUNKS, 34)), dma((CHUNKS + 1,)), dma((CHUNKS + 1,)),
            dma((CHIPS,)), dma((CHIPS,)),
        ],
        compiler_params=pltpu.CompilerParams(
            collective_id=0, has_side_effects=True, vmem_limit_bytes=48 * 2**20),
        cost_estimate=pl.CostEstimate(
            flops=16 * TOKENS * WIDTH * HID, bytes_accessed=12 * WIDTH * HID, transcendentals=OWN * HID),
    )(*placed)
    held = [pltpu.with_memory_space_constraint(v, pltpu.VMEM) for v in held]
    return pl.pallas_call(
        store,
        out_shape=tuple(jax.ShapeDtypeStruct(shape, BF) for shape in RESULTS),
        in_specs=[any_space] * 4,
        out_specs=(any_space,) * 4,
        scratch_shapes=[dma((4,))],
        compiler_params=pltpu.CompilerParams(vmem_limit_bytes=2**20),
    )(*held)


def solution(mesh):
    placed = (P("col", "row"), P("col", "row"), P("row", "col"), P("row", "col"), P("col", "row"))
    return jax.shard_map(
        body,
        mesh=mesh,
        in_specs=placed,
        out_specs=(P("col", "row"), P("row", "col"), P("row", "col"), P("col", "row")),
        check_vma=False,
    )
```

```python
import functools

import jax
import jax.numpy as jnp
from jax import lax
from jax.experimental import pallas as pl
from jax.experimental.pallas import tpu as pltpu
from jax.sharding import PartitionSpec as P

MESH = pl.DeviceIdType.MESH
BF = jnp.bfloat16
F32 = jnp.float32

RING = 4
CHIPS = 8
CORES = 2
CHUNKS = 4
OWN = 64
SUB = 16
WIDTH = 512
HID = 1792
HALF = HID // 2
CAT = 3 * HALF
TOKENS = 1024

CHIP_OF = (0, 1, 2, 5, 3, 4, 6, 7)
PLACE_OF = tuple(CHIP_OF.index(step) for step in range(CHIPS))
CHIP_ROWS = CORES * OWN
LAST = 0
HIDDEN, GRADS = slice(0, HALF), slice(HALF, CAT)
RESULTS = ((OWN, WIDTH), (WIDTH, HID), (WIDTH, HID), (HID, WIDTH))

ORDER = (
    ("first", 0), ("zf2", 9), ("rs_a1", 0), ("fwd1", 1), ("far4", 9), ("part", 1), ("zf3", 9), ("rs_a2", 0),
    ("far67", 9), ("rs_a1", 1), ("rs_b1", 0), ("fwd2", 2), ("part", 2), ("fwd3", 3), ("part", 3), ("rs_a2", 1),
    ("rs_b2", 0), ("rs_b1", 1), ("rs_a1", 3), ("rs_b2", 1), ("rs_a1", 2), ("ag_b1", 1), ("rs_a2", 3), ("ag_b2", 1),
    ("rs_b1", 3), ("rs_a2", 2), ("rs_b2", 3), ("ag_a1", 1), ("rs_b1", 2), ("ag_b1", 3), ("rs_b2", 2), ("ag_b2", 3),
    ("ag_b1", 0), ("ag_b1", 2), ("ag_a1", 3), ("ag_b2", 2), ("ag_a2", 1), ("in_part", 1), ("in_send", 1),
    ("ag_a1", 2), ("ag_a2", 3), ("ag_b2", 0), ("in_part", 3), ("ag_a2", 2), ("in_send", 3), ("in_part", 2),
    ("acc_g", 0), ("ag_a1", 0), ("in_send", 2), ("acc_u", 0), ("acc_u", 1), ("acc_g", 1), ("acc_d", 1), ("acc_d", 0),
    ("drain", 8), ("ag_a2", 0),
)


def dot(left, right, dims):
    return lax.dot_general(left, right, (dims, ((), ())), preferred_element_type=F32)


def kernel(
    tok_in, grd_in, wg_in, wu_in, wd_in, ing_ref, out_g, out_u, out_d,
    tok, grd, tok_t, hid_t, wg, wu, wd, part, gath, relay_a, land_a, relay_b, land_b,
    in_own, in_sib, in_far,
    load_sem, z_send, z_recv, f_send, f_recv, send, recv, i_send, i_recv, j_send, j_recv,
):
    row, col = lax.axis_index("row"), lax.axis_index("col")
    x, y = row % RING, row // RING
    z, core = col // CORES, col % CORES
    pa, pb = x + core * (y - x), y + core * (x - y)
    step_a, step_b = 1 + 3 * core, RING - 3 * core

    def at(a, b):
        return (a * step_a + b * step_b, col)

    up_a, down_a, opp_a = (pa + 1) % RING, (pa + 3) % RING, (pa + 2) % RING
    up_b, down_b, opp_b = (pb + 1) % RING, (pb + 3) % RING, (pb + 2) % RING
    dev_up_a, dev_down_a = at(up_a, pb), at(down_a, pb)
    dev_up_b, dev_down_b = at(pa, up_b), at(pa, down_b)
    sibling = (row, z * CORES + 1 - core)

    def far(step):
        return (row, ((z + step) % CHIPS) * CORES + core)

    loads = [
        pltpu.make_async_copy(tok_in, tok.at[0, core], load_sem.at[0]),
        pltpu.make_async_copy(grd_in, grd.at[0, core], load_sem.at[1]),
        pltpu.make_async_copy(wg_in, wg, load_sem.at[2]),
        pltpu.make_async_copy(wu_in, wu, load_sem.at[3]),
        pltpu.make_async_copy(wd_in, wd, load_sem.at[4]),
    ]
    for copy in loads:
        copy.start()

    barrier = pltpu.get_barrier_semaphore()
    peers = [dev_up_a, dev_down_a, dev_up_b, dev_down_b, sibling] + [far(s) for s in range(1, CHIPS)]
    for peer in peers:
        pl.semaphore_signal(barrier, inc=1, device_id=peer, device_id_type=MESH)
    pl.semaphore_wait(barrier, len(peers))

    started = []

    def push(src, dst, send_sem, recv_sem, device):
        copy = pltpu.make_async_remote_copy(
            src_ref=src, dst_ref=dst, send_sem=send_sem, recv_sem=recv_sem,
            device_id=device, device_id_type=MESH,
        )
        copy.start()
        started.append(copy)
        return copy

    from_sib, from_far = {}, {}

    def to_sibling(slot, src_tok, src_grd):
        from_sib[slot] = [
            push(src_tok, tok.at[slot, core], f_send.at[slot, 0], f_recv.at[slot, 0], sibling),
            push(src_grd, grd.at[slot, core], f_send.at[slot, 1], f_recv.at[slot, 1], sibling),
        ]

    def to_far(step):
        slot, device = PLACE_OF[step], far(CHIPS - step)
        from_far[slot] = [
            push(tok_in, tok.at[slot, core], z_send.at[slot, 0], z_recv.at[slot, 0], device),
            push(grd_in, grd.at[slot, core], z_send.at[slot, 1], z_recv.at[slot, 1], device),
        ]

    def relay_far(step):
        place, after = PLACE_OF[step], PLACE_OF[step + 1]
        from_far[after] = [
            push(tok.at[place, core], tok.at[after, core], z_send.at[after, 0], z_recv.at[after, 0], far(CHIPS - 1)),
            push(grd.at[place, core], grd.at[after, core], z_send.at[after, 1], z_recv.at[after, 1], far(CHIPS - 1)),
        ]

    def forward(slot):
        for copy in from_far[slot]:
            copy.wait_recv()
        to_sibling(slot, tok.at[slot, core], grd.at[slot, core])

    to_far(1)
    to_sibling(0, tok_in, grd_in)
    to_far(5)

    def settle(slot):
        for copy in from_sib[slot]:
            copy.wait_recv()

    def partial(j, first, count, ready=lambda i: None):
        slot, rows = 2 * j + first, count * CHIP_ROWS
        tokens = tok[slot:slot + count].reshape(rows, WIDTH)
        grads = grd[slot:slot + count].reshape(rows, WIDTH)
        for h in range(2):
            cols = slice(h * HALF, (h + 1) * HALF)

            def put(place, value):
                value = value.astype(BF)
                for i in range(count):
                    sub = 2 * (first + i)
                    part[j, h, :, sub:sub + 2, :, place * HALF:(place + 1) * HALF] = (
                        value[i * CHIP_ROWS:(i + 1) * CHIP_ROWS].reshape(RING, 2, SUB, HALF))

            if h == 0:
                ready(0)
            put(0, dot(tokens, wg[:, cols], ((1,), (0,))))
            if h == 0:
                ready(1)
            put(1, dot(tokens, wu[:, cols], ((1,), (0,))))
            if h == 0:
                ready(2)
            put(2, dot(grads, wd[cols, :], ((1,), (1,))))

    def turn(j):
        chips = [tok[2 * j + i].reshape(CHIP_ROWS, WIDTH) for i in range(2)]
        rows = [chips[i][32 * b:32 * b + 32] for b in range(RING) for i in range(2)]
        tok_t[:, j * 256:(j + 1) * 256] = jnp.concatenate(rows, axis=0).T

    def scatter_start(j, base, view, relay, land, me_up, me_down, me_opp, to_up, to_down):
        return {
            "r0": [push(view(0, me_opp), relay(0), send.at[j, base], recv.at[j, base], to_up)],
            "r1": [push(view(1, me_opp), relay(1), send.at[j, base + 1], recv.at[j, base + 1], to_down)],
            "u1": [push(view(1, me_up), land(0, 1), send.at[j, base + 2], recv.at[j, base + 2], to_up)],
            "d0": [push(view(0, me_down), land(1, 0), send.at[j, base + 3], recv.at[j, base + 3], to_down)],
        }

    def settle_all(copies, *names):
        for name in names:
            for copy in copies[name]:
                copy.wait_recv()

    def scatter_relay(j, base, copies, view, add, land, me_up, me_down, to_up, to_down):
        settle_all(copies, "r0")
        add(0, me_up)
        copies["u0"] = [push(view(0, me_up), land(0, 0), send.at[j, base + 4], recv.at[j, base + 4], to_up)]
        settle_all(copies, "r1")
        add(1, me_down)
        copies["d1"] = [push(view(1, me_down), land(1, 1), send.at[j, base + 5], recv.at[j, base + 5], to_down)]

    def settle_scatter(copies):
        settle_all(copies, "u1", "d0", "u0", "d1")

    def gather_start(j, base, view, to_up, to_down):
        return {
            "u0": push(view(0), view(0), send.at[j, base], recv.at[j, base], to_up),
            "d1": push(view(1), view(1), send.at[j, base + 1], recv.at[j, base + 1], to_down),
            "u1": push(view(1), view(1), send.at[j, base + 2], recv.at[j, base + 2], to_up),
            "d0": push(view(0), view(0), send.at[j, base + 3], recv.at[j, base + 3], to_down),
        }

    def gather_relay(j, base, copies, view_down, view_up, to_up, to_down):
        copies["u0"].wait_recv()
        copies["f0"] = push(view_down(0), view_down(0), send.at[j, base + 4], recv.at[j, base + 4], to_up)
        copies["d1"].wait_recv()
        copies["f1"] = push(view_up(1), view_up(1), send.at[j, base + 5], recv.at[j, base + 5], to_down)

    def settle_gather(copies):
        for name in ("u1", "d0", "f0", "f1"):
            copies[name].wait_recv()

    state = {}

    def view_a(j):
        return lambda h, block: part.at[j, h, block]

    def view_b(j):
        return lambda h, block: part.at[j, h, pa, block]

    def land_view(land, j):
        return lambda side, h: land.at[j, side, h]

    def relay_view(relay, j):
        return lambda h: relay.at[j, h]

    def begin(j):
        state["ra", j] = scatter_start(
            j, 0, view_a(j), relay_view(relay_a, j), land_view(land_a, j), up_a, down_a, opp_a, dev_up_a, dev_down_a)

    def begin_half(j, i):
        subs = slice(2 * i, 2 * i + 2)
        copies = scatter_start(
            j, 24 if i else 0, lambda h, block: part.at[j, h, block, subs], lambda h: relay_a.at[j, h, subs],
            lambda side, h: land_a.at[j, side, h, subs], up_a, down_a, opp_a, dev_up_a, dev_down_a)
        if i:
            copies = {name: state["ra", j][name] + copies[name] for name in copies}
        state["ra", j] = copies

    def relay_half(i):
        copies = state["ra", 0]
        ways = (
            ("r0", 0, up_a, "u0", 0, dev_up_a, 34 if i else 4),
            ("r1", 1, down_a, "d1", 1, dev_down_a, 35 if i else 5),
        )
        for came, h, block, goes, side, device, sem in ways:
            copies[came][i].wait_recv()
            for sub in (2 * i, 2 * i + 1):
                total = part[0, h, block, sub].astype(F32) + relay_a[0, h, sub].astype(F32)
                part[0, h, block, sub] = total.astype(BF)
            subs = slice(2 * i, 2 * i + 2)
            copies.setdefault(goes, []).append(push(
                part.at[0, h, block, subs], land_a.at[0, side, h, subs], send.at[0, sem], recv.at[0, sem], device))

    def op_first(j):
        loads[0].wait()
        loads[1].wait()
        settle(0)
        partial(0, 0, 1, lambda i: loads[2 + i].wait())
        begin_half(0, 0)
        forward(1)
        relay_far(1)
        settle(1)
        partial(0, 1, 1)
        begin_half(0, 1)
        relay_half(0)
        turn(0)

    def op_zf2(j):
        forward(PLACE_OF[2])
        relay_far(2)

    def op_far4(j):
        to_far(4)

    def op_zf3(j):
        forward(PLACE_OF[3])

    def op_far67(j):
        to_far(6)
        to_far(7)

    def op_fwd1(j):
        forward(PLACE_OF[5])

    def op_fwd2(j):
        forward(PLACE_OF[4])

    def op_fwd3(j):
        forward(PLACE_OF[7])
        forward(PLACE_OF[6])

    def op_part(j):
        settle(2 * j)
        settle(2 * j + 1)
        partial(j, 0, 2)
        begin(j)
        turn(j)

    def op_rs_a1(j):
        if j == 0:
            relay_half(1)
            return

        def add(h, block):
            def some(i, carry):
                total = part[j, h, block, i].astype(F32) + relay_a[j, h, i].astype(F32)
                part[j, h, block, i] = total.astype(BF)
                return carry
            lax.fori_loop(0, RING, some, 0)
        scatter_relay(
            j, 0, state["ra", j], view_a(j), add, land_view(land_a, j), up_a, down_a, dev_up_a, dev_down_a)

    def op_rs_a2(j):
        settle_scatter(state["ra", j])
        for h in range(2):
            def some(i, carry):
                total = part[j, h, pa, i].astype(F32) + land_a[j, 0, h, i].astype(F32)
                part[j, h, pa, i] = (total + land_a[j, 1, h, i].astype(F32)).astype(BF)
                return carry
            lax.fori_loop(0, RING, some, 0)
        state["rb", j] = scatter_start(
            j, 6, view_b(j), relay_view(relay_b, j), land_view(land_b, j), up_b, down_b, opp_b, dev_up_b, dev_down_b)

    def op_rs_b1(j):
        def add(h, block):
            total = part[j, h, pa, block].astype(F32) + relay_b[j, h].astype(F32)
            part[j, h, pa, block] = total.astype(BF)
        scatter_relay(
            j, 6, state["rb", j], view_b(j), add, land_view(land_b, j), up_b, down_b, dev_up_b, dev_down_b)

    def op_rs_b2(j):
        settle_scatter(state["rb", j])
        for h in range(2):
            def total(place):
                cols = slice(place * HALF, (place + 1) * HALF)
                value = part[j, h, pa, pb, :, cols].astype(F32) + land_b[j, 0, h, :, cols].astype(F32)
                value = value + land_b[j, 1, h, :, cols].astype(F32)
                return value.astype(BF).astype(F32)
            g_val, u_val, d_val = total(0), total(1), total(2)
            sig = 1.0 / (1.0 + jnp.exp(-g_val))
            act = g_val * sig
            gath[h, j, pa, pb, :, 0:HALF] = (act * u_val).astype(BF)
            gath[h, j, pa, pb, :, HALF:2 * HALF] = (d_val * u_val * sig * (1.0 + g_val * (1.0 - sig))).astype(BF)
            gath[h, j, pa, pb, :, 2 * HALF:] = (d_val * act).astype(BF)
        state["gb", j] = gather_start(j, 12, lambda h: gath.at[h, j, pa, pb], dev_up_b, dev_down_b)

    def op_ag_b1(j):
        gather_relay(
            j, 12, state["gb", j], lambda h: gath.at[h, j, pa, down_b], lambda h: gath.at[h, j, pa, up_b],
            dev_up_b, dev_down_b)

    def view_last(cols):
        return lambda h, block=None: gath.at[h, LAST, pa if block is None else block, :, :, cols]

    def op_ag_b2(j):
        settle_gather(state["gb", j])
        if j == LAST:
            state["ga", j] = gather_start(j, 18, view_last(GRADS), dev_up_a, dev_down_a)
            return
        state["ga", j] = gather_start(j, 18, lambda h: gath.at[h, j, pa], dev_up_a, dev_down_a)

    def op_ag_a1(j):
        if j == LAST:
            view = view_last(GRADS)
            gather_relay(
                j, 18, state["ga", j], lambda h: view(h, down_a), lambda h: view(h, up_a), dev_up_a, dev_down_a)
            state["gh", j] = gather_start(j, 28, view_last(HIDDEN), dev_up_a, dev_down_a)
            return
        gather_relay(
            j, 18, state["ga", j], lambda h: gath.at[h, j, down_a], lambda h: gath.at[h, j, up_a],
            dev_up_a, dev_down_a)

    def op_ag_h(j):
        view = view_last(HIDDEN)
        gather_relay(
            j, 28, state["gh", j], lambda h: view(h, down_a), lambda h: view(h, up_a), dev_up_a, dev_down_a)

    def op_ag_a2(j):
        settle_gather(state["ga", j])

    def gathered(h, j, place):
        cols = slice(place * HALF, (place + 1) * HALF)
        chips = [gath[h, j, :, 2 * i:2 * i + 2, :, cols].reshape(CHIP_ROWS, HALF) for i in range(2)]
        return jnp.concatenate(chips, axis=0)

    def in_half(j, i):
        total = None
        for h in range(2):
            cols = slice(h * HALF, (h + 1) * HALF)
            for place, weight in ((1, wg), (2, wu)):
                value = gath[h, j, :, 2 * i:2 * i + 2, :, place * HALF:(place + 1) * HALF].reshape(CHIP_ROWS, HALF)
                term = dot(value, weight[:, cols], ((1,), (1,)))
                total = term if total is None else total + term
        slot = 2 * j + i
        in_own[slot] = total.astype(BF).reshape(CORES, OWN, WIDTH)
        sem = j if i else CHUNKS
        return push(in_own.at[slot, 1 - core], in_sib.at[slot], i_send.at[sem], i_recv.at[sem], sibling)

    def pair(slot):
        value = in_own[slot, core].astype(F32) + in_sib[slot].astype(F32)
        in_own[slot, core] = value.astype(BF)
        if slot:
            state["iz", slot] = push(
                in_own.at[slot, core], in_far.at[slot], j_send.at[slot], j_recv.at[slot], far(CHIP_OF[slot]))

    def turn_hidden(j):
        for h in range(2):
            hid_t[h, :, j * 256:(j + 1) * 256] = gathered(h, j, 0).T

    def op_in_part(j):
        total = None
        for h in range(2):
            cols = slice(h * HALF, (h + 1) * HALF)
            for place, weight in ((1, wg), (2, wu)):
                term = dot(gathered(h, j, place), weight[:, cols], ((1,), (1,)))
                total = term if total is None else total + term
        in_own[2 * j:2 * j + 2] = total.astype(BF).reshape(2, CORES, OWN, WIDTH)
        state["is", j] = push(
            in_own.at[2 * j:2 * j + 2, 1 - core], in_sib.at[2 * j:2 * j + 2], i_send.at[j], i_recv.at[j], sibling)
        turn_hidden(j)

    def op_in_send(j):
        state["is", j].wait_recv()
        for slot in sorted((2 * j, 2 * j + 1), key=lambda p: -min(CHIP_OF[p], CHIPS - CHIP_OF[p])):
            pair(slot)

    def grads_of(h, place, j, count, out, more=False):
        cols = slice(h * HALF, (h + 1) * HALF)
        rows = slice(j * 256, (j + count) * 256)
        value = gath[h, j:j + count, :, :, :, place * HALF:(place + 1) * HALF].reshape(count * 256, HALF)
        term = dot(tok_t[:, rows], value, ((1,), (0,)))
        if more:
            term = out[:, cols].astype(F32) + term
        out[:, cols] = term.astype(BF)

    def down_of(h, j, count, more=False):
        cols = slice(h * HALF, (h + 1) * HALF)
        rows = slice(j * 256, (j + count) * 256)
        grads = grd[2 * j:2 * (j + count)].reshape(count * 256, WIDTH)
        term = dot(hid_t[h, :, rows], grads, ((1,), (0,)))
        if more:
            term = out_d[cols, :].astype(F32) + term
        out_d[cols, :] = term.astype(BF)

    waited = []

    def op_drain(count):
        for copy in started[len(waited):len(started) - count]:
            copy.wait_send()
            waited.append(copy)

    def op_acc_g(h):
        grads_of(h, 1, 2, 2, out_g)

    def op_acc_u(h):
        grads_of(h, 2, 2, 2, out_u)

    def op_acc_d(h):
        down_of(h, 2, 2)

    ops = dict(
        acc_g=op_acc_g, acc_u=op_acc_u, acc_d=op_acc_d, drain=op_drain,
        first=op_first, zf2=op_zf2, zf3=op_zf3, far4=op_far4, far67=op_far67, fwd1=op_fwd1, fwd2=op_fwd2, fwd3=op_fwd3,
        part=op_part, rs_a1=op_rs_a1, rs_a2=op_rs_a2, rs_b1=op_rs_b1, rs_b2=op_rs_b2,
        ag_b1=op_ag_b1, ag_b2=op_ag_b2, ag_a1=op_ag_a1, ag_a2=op_ag_a2, in_part=op_in_part, in_send=op_in_send,
    )
    for name, j in ORDER:
        ops[name](j)

    near = in_half(LAST, 1)
    op_ag_h(LAST)
    own = in_half(LAST, 0)
    near.wait_recv()
    pair(1)
    for h in range(2):
        grads_of(h, 1, 0, 2, out_g, True)
    for h in range(2):
        grads_of(h, 2, 0, 2, out_u, True)
    own.wait_recv()
    pair(0)
    settle_gather(state["gh", LAST])
    turn_hidden(LAST)
    for h in range(2):
        down_of(h, 0, 2, True)

    total = in_own[0, core].astype(F32)
    for slot in range(1, CHIPS):
        state["iz", slot].wait_recv()
        total = total + in_far[slot].astype(F32)
    ing_ref[...] = total.astype(BF)

    op_drain(0)


def store(*refs):
    sems = refs[-1]
    copies = [pltpu.make_async_copy(refs[i], refs[4 + i], sems.at[i]) for i in range(4)]
    for copy in copies:
        copy.start()
    for copy in copies:
        copy.wait()


def body(tokens, out_grad, w_gate, w_up, w_down):
    any_space = pl.BlockSpec(memory_space=pl.ANY)
    dma = pltpu.SemaphoreType.DMA
    vmem = pltpu.VMEM
    placed = [pltpu.with_memory_space_constraint(v, pltpu.HBM) for v in (tokens, out_grad, w_gate, w_up, w_down)]
    held = pl.pallas_call(
        kernel,
        out_shape=tuple(vmem(shape, BF) for shape in RESULTS),
        in_specs=[pl.BlockSpec(memory_space=pltpu.HBM)] * 5,
        out_specs=(pl.BlockSpec(memory_space=pltpu.VMEM),) * 4,
        scratch_shapes=[
            vmem((CHIPS, CORES, OWN, WIDTH), BF),
            vmem((CHIPS, CORES, OWN, WIDTH), BF),
            vmem((WIDTH, TOKENS), BF),
            vmem((2, HALF, TOKENS), BF),
            vmem((WIDTH, HID), BF),
            vmem((WIDTH, HID), BF),
            vmem((HID, WIDTH), BF),
            vmem((CHUNKS, 2, RING, RING, SUB, CAT), BF),
            vmem((2, CHUNKS, RING, RING, SUB, CAT), BF),
            vmem((CHUNKS, 2, RING, SUB, CAT), BF),
            vmem((CHUNKS, 2, 2, RING, SUB, CAT), BF),
            vmem((CHUNKS, 2, SUB, CAT), BF),
            vmem((CHUNKS, 2, 2, SUB, CAT), BF),
            vmem((CHIPS, CORES, OWN, WIDTH), BF),
            vmem((CHIPS, OWN, WIDTH), BF),
            vmem((CHIPS, OWN, WIDTH), BF),
            dma((5,)), dma((CHIPS, 2)), dma((CHIPS, 2)), dma((CHIPS, 2)), dma((CHIPS, 2)),
            dma((CHUNKS, 36)), dma((CHUNKS, 36)), dma((CHUNKS + 1,)), dma((CHUNKS + 1,)),
            dma((CHIPS,)), dma((CHIPS,)),
        ],
        compiler_params=pltpu.CompilerParams(
            collective_id=0, has_side_effects=True, vmem_limit_bytes=48 * 2**20),
        cost_estimate=pl.CostEstimate(
            flops=16 * TOKENS * WIDTH * HID, bytes_accessed=12 * WIDTH * HID, transcendentals=OWN * HID),
    )(*placed)
    held = [pltpu.with_memory_space_constraint(v, pltpu.VMEM) for v in held]
    return pl.pallas_call(
        store,
        out_shape=tuple(jax.ShapeDtypeStruct(shape, BF) for shape in RESULTS),
        in_specs=[any_space] * 4,
        out_specs=(any_space,) * 4,
        scratch_shapes=[dma((4,))],
        compiler_params=pltpu.CompilerParams(vmem_limit_bytes=2**20),
    )(*held)


def solution(mesh):
    placed = (P("col", "row"), P("col", "row"), P("row", "col"), P("row", "col"), P("col", "row"))
    return jax.shard_map(
        body,
        mesh=mesh,
        in_specs=placed,
        out_specs=(P("col", "row"), P("row", "col"), P("row", "col"), P("col", "row")),
        check_vma=False,
    )
```
